256 devices in a mesh: frame: 16 (over y, z_hi), row: 16 (over z_lo, x, core).
Axes of the slice: x: 4, y: 4, z: 8 (z_hi: 4, z_lo: 2; z = z_hi * 2 + z_lo), core: 2. Of those that a mesh axis runs over, the one named last changes fastest.
Arguments:
- frames_x: bfloat16 [16, 96, 128, 512], P('frame', 'row'), may hold values from -6 to 6
- conv_weight: bfloat16 [3, 3, 512, 512], replicated, may hold values from -0.09375 to 0.09375
- conv_bias: float32 [512], replicated, may hold values from -3 to 3
- query_weight: bfloat16 [512, 512], replicated, may hold values from -0.25 to 0.25
- key_weight: bfloat16 [512, 512], replicated, may hold values from -0.25 to 0.25
- value_weight: bfloat16 [512, 512], replicated, may hold values from -0.25 to 0.25
- out_weight: bfloat16 [512, 512], replicated, may hold values from -0.25 to 0.25
- query_gain: float32 [512], replicated, may hold values from 0.5 to 2
- key_gain: float32 [512], replicated, may hold values from 0.5 to 2
- source_ids: int32 [16, 96, 4], P('frame', 'row'), may hold values from 0 to 95, as said below
- valid_counts: int32 [16, 96], P('frame', 'row'), may hold values from 1 to 4
Outputs:
- propagated: bfloat16 [16, 96, 128, 512], P('frame', 'row')
The draws below stay inside these ranges and needn't reach their ends.
Inputs may be any that keep to these rules, and one draw needn't show every extreme that they name: `source_ids`: block id s names row s // 1 of the previous frame, which lies at most 2 rows from the querying block's row; in every frame slot 0 of the blocks in even rows names a block 2 rows above and in odd rows 2 rows below, as far as the frame has that row.
All inputs are finite; a program needn't handle non-finite values.
Results may differ from the reference program's by a relative error of at most 0.0054.
Values may be sent and summed in bfloat16 or wider, within the bound.
No kernel may reach another device: no remote copies, remote signals or barrier semaphores. Data moves between devices by JAX's collectives and lax.ppermute only.
A program may use at most 64 MiB of HBM per device.

```python
import math
import jax
import jax.numpy as jnp
from jax import lax

HEADS = 8
HD = 64
C = 512
KSRC = 4
BLOCK = 128
DISP = 2
W = 128
FRAMES = 16
H = 96
BPR = 1
NB = 96


def draw_source_ids(key, part):
    first_key, second_key = jax.random.split(jax.random.fold_in(key, 11))
    block_rows = jnp.arange(NB, dtype=jnp.int32) // BPR
    offsets = jax.random.randint(first_key, (FRAMES, NB, KSRC - 1), -DISP, DISP + 1)
    leading = jnp.where(block_rows % 2 == 0, -DISP, DISP).astype(jnp.int32)
    leading = jnp.broadcast_to(leading[None, :, None], (FRAMES, NB, 1))
    offsets = jnp.concatenate([leading, offsets.astype(jnp.int32)], axis=2)
    source_rows = jnp.clip(block_rows[None, :, None] + offsets, 0, H - 1)
    columns = jax.random.randint(second_key, (FRAMES, NB, KSRC), 0, BPR)
    return (source_rows * BPR + columns).astype(jnp.int32)


def plant(drawn, own_key, low, high):
    longest = drawn.shape.index(max(drawn.shape))
    spots = []
    for shift in (0, 1):
        where = [jax.random.randint(jax.random.fold_in(own_key, axis), (), 0, length) for axis, length in enumerate(drawn.shape)]
        where[longest] = (where[longest] + shift) % drawn.shape[longest]
        spots.append(tuple(where))
    return drawn.at[spots[0]].set(low).at[spots[1]].set(high)


def block_scale(stream_key, shape, shards, smallest, high):
    def one(position, blocks):
        draws = jax.random.uniform(jax.random.fold_in(jax.random.fold_in(stream_key, 6), position), (blocks,), jnp.float32, smallest / len(shards), high / len(shards))
        return jnp.repeat(jnp.exp(draws), shape[position] // blocks).reshape((-1,) + (1,) * (len(shape) - position - 1))

    factor_of = one(*shards[0])
    for cut in shards[1:]:
        factor_of = factor_of * one(*cut)
    return factor_of


def centred(own_key, extent, deviation, most, pieces=(), kind=jnp.bfloat16):
    array = deviation * jax.random.normal(own_key, extent, jnp.float32)
    if pieces:
        array = array * block_scale(own_key, extent, pieces, -0.22, 0.18)
    return jnp.clip(array, -most, most).astype(kind)


def setup_inputs(seed: int = 0) -> dict:
    streams_of = jax.random.split(jax.random.key(seed), 12)
    return {
        "frames_x": centred(streams_of[0], (FRAMES, H, W, C), 1.0, 6.0, ((0, 16), (1, 16))),
        "conv_weight": centred(streams_of[1], (3, 3, C, C), (9 * C) ** -0.5, 0.09375),
        "conv_bias": centred(streams_of[2], (C,), 0.5, 3.0, (), jnp.float32),
        "query_weight": centred(streams_of[3], (C, C), C ** -0.5, 0.25),
        "key_weight": centred(streams_of[4], (C, C), C ** -0.5, 0.25),
        "value_weight": centred(streams_of[5], (C, C), C ** -0.5, 0.25),
        "out_weight": centred(streams_of[6], (C, C), C ** -0.5, 0.25),
        "query_gain": jnp.clip(jnp.exp(jax.random.uniform(streams_of[7], (C,), jnp.float32, math.log(0.5), math.log(2.0))), 0.5, 2.0),
        "key_gain": jnp.clip(jnp.exp(jax.random.uniform(streams_of[8], (C,), jnp.float32, math.log(0.5), math.log(2.0))), 0.5, 2.0),
        "source_ids": draw_source_ids(jax.random.fold_in(streams_of[11], 71), 0),
        "valid_counts": plant(jax.random.randint(streams_of[10], (FRAMES, NB), 1, 5), jax.random.fold_in(streams_of[10], 1), 1, 4).astype(jnp.int32),
    }


def conv_frame(frame_in, conv_weight, conv_bias):
    padded = jnp.pad(frame_in, ((1, 1), (1, 1), (0, 0)))
    total = jnp.zeros((H * W, C), jnp.float32)
    for row_off in range(3):
        for col_off in range(3):
            window = padded[row_off:row_off + H, col_off:col_off + W].reshape(H * W, C)
            total = total + jnp.dot(window, conv_weight[row_off, col_off], preferred_element_type=jnp.float32)
    return (total + conv_bias).astype(jnp.bfloat16)

def normed(feats, weight, gain):
    proj = jnp.dot(feats, weight, preferred_element_type=jnp.float32).reshape(-1, HEADS, HD)
    proj = proj * lax.rsqrt(lax.optimization_barrier(jnp.mean(proj * proj, axis=-1, keepdims=True)) + 1e-06) * gain.reshape(HEADS, HD)
    return proj.reshape(-1, C).astype(jnp.bfloat16)

def attend(queries, key_set, value_set, mask):
    count = queries.shape[0]
    query_heads = queries.reshape(count, BLOCK, HEADS, HD).astype(jnp.float32)
    key_heads = key_set.reshape(count, -1, HEADS, HD).astype(jnp.float32)
    value_heads = value_set.reshape(count, -1, HEADS, HD).astype(jnp.float32)
    scores = jnp.einsum('nqhd,nkhd->nhqk', query_heads, key_heads) * HD ** (-0.5)
    expo = jnp.where(mask[:, None, None, :], jnp.exp(scores), 0.0)
    probs = (expo / lax.optimization_barrier(jnp.sum(expo, axis=-1, keepdims=True))).astype(jnp.bfloat16)
    mixed = jnp.einsum('nhqk,nkhd->nqhd', probs.astype(jnp.float32), value_heads)
    return mixed.reshape(count * BLOCK, C).astype(jnp.bfloat16)

def reference(frames_x, conv_weight, conv_bias, query_weight, key_weight, value_weight, out_weight, query_gain, key_gain, source_ids, valid_counts):
    feats_all = lax.map(lambda one: conv_frame(one, conv_weight, conv_bias), frames_x)
    queries_all = lax.map(lambda one: normed(one, query_weight, query_gain), feats_all)
    keys_all = lax.map(lambda one: normed(one, key_weight, key_gain), feats_all)
    values_all = lax.map(lambda one: jnp.dot(one, value_weight, preferred_element_type=jnp.float32).astype(jnp.bfloat16), feats_all)

    def one_frame(frame_pos):
        earlier = jnp.maximum(frame_pos - 1, 0)
        prev_keys = keys_all[earlier].reshape(NB, BLOCK, C)
        prev_values = values_all[earlier].reshape(NB, BLOCK, C)
        chosen = source_ids[frame_pos]
        key_set = jnp.concatenate([keys_all[frame_pos].reshape(NB, 1, BLOCK, C), prev_keys[chosen]], axis=1).reshape(NB, -1, C)
        value_set = jnp.concatenate([values_all[frame_pos].reshape(NB, 1, BLOCK, C), prev_values[chosen]], axis=1).reshape(NB, -1, C)
        slots = (jnp.arange(KSRC, dtype=jnp.int32)[None, :] < valid_counts[frame_pos][:, None]) & (frame_pos > 0)
        slot_mask = jnp.concatenate([jnp.ones((NB, 1), dtype=bool), slots], axis=1)
        mask = jnp.repeat(slot_mask, BLOCK, axis=1)
        mixed = attend(queries_all[frame_pos].reshape(NB, BLOCK, C), key_set, value_set, mask)
        result = feats_all[frame_pos].astype(jnp.float32) + jnp.dot(mixed, out_weight, preferred_element_type=jnp.float32)
        return result.astype(jnp.bfloat16).reshape(H, W, C)
    return lax.map(one_frame, jnp.arange(FRAMES, dtype=jnp.int32))
```

```python
import functools

import jax
import jax.numpy as jnp
from jax import lax
from jax.experimental import pallas as pl
from jax.experimental.pallas import tpu as pltpu
from jax.sharding import PartitionSpec as P

HEADS = 8
HD = 64
KSRC = 4
BLOCK = 128
DISP = 2
PAIR = 2 * HD
VMEM_BYTES = 48 * 1024 * 1024

NT = (((1,), (1,)), ((), ()))


def dot(a, b):
    return jnp.dot(a, b, preferred_element_type=jnp.float32)


def shifted_sum(y_left, y_mid, y_right):
    tokens = y_mid.shape[0]
    column = lax.broadcasted_iota(jnp.int32, y_mid.shape, 0) % BLOCK
    left = jnp.where(column == 0, 0.0, pltpu.roll(y_left, 1, 0))
    right = jnp.where(column == BLOCK - 1, 0.0, pltpu.roll(y_right, tokens - 1, 0))
    return left + y_mid + right


def conv_inner_kernel(x_ref, w_ref, b_ref, out_ref, acc_ref):
    tokens = out_ref.shape[0]
    step = pl.program_id(0)
    y = sum(dot(x_ref[pl.ds(a * BLOCK, tokens)], w_ref[a, 0]) for a in range(3))
    column = lax.broadcasted_iota(jnp.int32, y.shape, 0) % BLOCK

    @pl.when(step == 0)
    def _():
        acc_ref[...] = jnp.where(column == 0, 0.0, pltpu.roll(y, 1, 0)) + b_ref[...]

    @pl.when(step == 1)
    def _():
        acc_ref[...] += y

    @pl.when(step == 2)
    def _():
        right = jnp.where(column == BLOCK - 1, 0.0, pltpu.roll(y, tokens - 1, 0))
        out_ref[...] = (acc_ref[...] + right).astype(jnp.bfloat16)


def conv_edge_kernel(before_ref, top_ref, bottom_ref, after_ref, w_ref, b_ref, out_ref, acc_ref):
    tokens = out_ref.shape[0]
    step = pl.program_id(0)
    upper = [before_ref[...], top_ref[pl.ds(0, BLOCK)], top_ref[pl.ds(BLOCK, BLOCK)]]
    lower = [bottom_ref[pl.ds(0, BLOCK)], bottom_ref[pl.ds(BLOCK, BLOCK)], after_ref[...]]
    y = sum(dot(jnp.concatenate([upper[a], lower[a]], 0), w_ref[a, 0]) for a in range(3))
    column = lax.broadcasted_iota(jnp.int32, y.shape, 0) % BLOCK

    @pl.when(step == 0)
    def _():
        acc_ref[...] = jnp.where(column == 0, 0.0, pltpu.roll(y, 1, 0)) + b_ref[...]

    @pl.when(step == 1)
    def _():
        acc_ref[...] += y

    @pl.when(step == 2)
    def _():
        right = jnp.where(column == BLOCK - 1, 0.0, pltpu.roll(y, tokens - 1, 0))
        out_ref[...] = (acc_ref[...] + right).astype(jnp.bfloat16)


def head_norm(proj, gain):
    squares = (proj * proj).astype(jnp.bfloat16)
    row = lax.broadcasted_iota(jnp.int32, (4 * HD, 4 * HD), 0) // HD
    col = lax.broadcasted_iota(jnp.int32, (4 * HD, 4 * HD), 1) // HD
    mean_of = jnp.where(row == col, 1.0 / HD, 0.0).astype(jnp.bfloat16)
    wide = 4 * HD
    means = [dot(squares[:, i : i + wide], mean_of) for i in range(0, HEADS * HD, wide)]
    mean = jnp.concatenate(means, 1)
    return (proj * lax.rsqrt(mean + 1e-06) * gain).astype(jnp.bfloat16)


def pair_product(q, k, v):
    low = lax.broadcasted_iota(jnp.int32, (BLOCK, PAIR), 1) < HD
    zero = jnp.zeros((BLOCK, PAIR), jnp.bfloat16)
    one = jnp.ones((BLOCK, PAIR), jnp.bfloat16)
    keys = jnp.concatenate([jnp.where(low, k, zero), jnp.where(low, zero, k)], 0)
    scores = lax.dot_general(q, keys, NT, preferred_element_type=jnp.float32)
    expo = jnp.exp(scores).astype(jnp.bfloat16)
    upper = jnp.concatenate([jnp.where(low, v, zero), jnp.where(low, one, zero)], 1)
    lower = jnp.concatenate([jnp.where(low, zero, v), jnp.where(low, zero, one)], 1)
    return dot(expo, jnp.concatenate([upper, lower], 0))


def own_kernel(f_ref, wq_ref, wk_ref, wv_ref, gq_ref, gk_ref, q_ref, sums_ref, norms_ref, k_ref, v_ref):
    feats = f_ref[...]
    q_ref[...] = head_norm(dot(feats, wq_ref[...]), gq_ref[...] * HD**-0.5)
    k_ref[...] = head_norm(dot(feats, wk_ref[...]), gk_ref[...])
    v_ref[...] = dot(feats, wv_ref[...]).astype(jnp.bfloat16)

    @pl.loop(0, f_ref.shape[0] // BLOCK)
    def _(block):
        rows = pl.ds(pl.multiple_of(block * BLOCK, BLOCK), BLOCK)
        for p in range(HEADS // 2):
            cols = pl.ds(p * PAIR, PAIR)
            both = pair_product(q_ref[rows, cols], k_ref[rows, cols], v_ref[rows, cols])
            sums_ref[rows, cols] = both[:, :PAIR]
            norms_ref[rows, cols] = both[:, PAIR:]


def last_kernel(
    ids_ref, counts_ref, up_ref, prev_ref, down_ref, f_ref, q_ref, sums_in_ref, norms_in_ref,
    wk_ref, wv_ref, wo_ref, gk_ref, out_ref, k_ref, v_ref, sums_ref, norms_ref,
):
    halo = DISP * BLOCK
    inner = prev_ref.shape[0]
    for ref, start in ((up_ref, 0), (prev_ref, halo), (down_ref, halo + inner)):
        feats = ref[...]
        rows = pl.ds(start, feats.shape[0])
        k_ref[rows] = head_norm(dot(feats, wk_ref[...]), gk_ref[...])
        v_ref[rows] = dot(feats, wv_ref[...]).astype(jnp.bfloat16)
    sums_ref[...] = sums_in_ref[...]
    norms_ref[...] = norms_in_ref[...]
    for block in range(f_ref.shape[0] // BLOCK):
        rows = pl.ds(block * BLOCK, BLOCK)

        @pl.loop(0, counts_ref[block])
        def _(slot):
            src = pl.ds(pl.multiple_of(ids_ref[block, slot] * BLOCK, BLOCK), BLOCK)
            for p in range(HEADS // 2):
                cols = pl.ds(p * PAIR, PAIR)
                both = pair_product(q_ref[rows, cols], k_ref[src, cols], v_ref[src, cols])
                sums_ref[rows, cols] += both[:, :PAIR]
                norms_ref[rows, cols] += both[:, PAIR:]

    mixed = (sums_ref[...] / norms_ref[...]).astype(jnp.bfloat16)
    result = f_ref[...].astype(jnp.float32) + dot(mixed, wo_ref[...])
    out_ref[...] = result.astype(jnp.bfloat16)


def params(**kw):
    return pltpu.CompilerParams(vmem_limit_bytes=VMEM_BYTES, **kw)


def cost(flops, moved):
    return pl.CostEstimate(flops=int(flops), bytes_accessed=int(moved), transcendentals=0)


def conv_inner(x, weight, bias):
    tokens, chans = x.shape[0] - 2 * BLOCK, x.shape[1]
    return pl.pallas_call(
        conv_inner_kernel,
        grid=(3,),
        in_specs=[
            pl.BlockSpec(x.shape, lambda i: (0, 0)),
            pl.BlockSpec((3, 1, chans, chans), lambda i: (0, i, 0, 0)),
            pl.BlockSpec((1, chans), lambda i: (0, 0)),
        ],
        out_specs=pl.BlockSpec((tokens, chans), lambda i: (0, 0)),
        out_shape=jax.ShapeDtypeStruct((tokens, chans), jnp.bfloat16),
        scratch_shapes=[pltpu.VMEM((tokens, chans), jnp.float32)],
        compiler_params=params(),
        cost_estimate=cost(18 * tokens * chans * chans, 2 * weight.size + 4 * x.size),
        name="conv_inner",
    )(x, weight, bias)


def conv_edge(before, x, after, weight, bias):
    tokens, chans = 2 * BLOCK, x.shape[1]
    last = x.shape[0] // tokens - 1
    return pl.pallas_call(
        conv_edge_kernel,
        grid=(3,),
        in_specs=[
            pl.BlockSpec((BLOCK, chans), lambda i: (0, 0)),
            pl.BlockSpec((tokens, chans), lambda i: (0, 0)),
            pl.BlockSpec((tokens, chans), lambda i: (last, 0)),
            pl.BlockSpec((BLOCK, chans), lambda i: (0, 0)),
            pl.BlockSpec((3, 1, chans, chans), lambda i: (0, i, 0, 0)),
            pl.BlockSpec((1, chans), lambda i: (0, 0)),
        ],
        out_specs=pl.BlockSpec((tokens, chans), lambda i: (0, 0)),
        out_shape=jax.ShapeDtypeStruct((tokens, chans), jnp.bfloat16),
        scratch_shapes=[pltpu.VMEM((tokens, chans), jnp.float32)],
        compiler_params=params(),
        cost_estimate=cost(18 * tokens * chans * chans, 2 * weight.size + 4 * x.size),
        name="conv_edge",
    )(before, x, x, after, weight, bias)


def own_part(feats, wq, wk, wv, gq, gk):
    tokens, chans = feats.shape
    return pl.pallas_call(
        own_kernel,
        out_shape=[
            jax.ShapeDtypeStruct((tokens, chans), jnp.bfloat16),
            jax.ShapeDtypeStruct((tokens, chans), jnp.float32),
            jax.ShapeDtypeStruct((tokens, chans), jnp.float32),
        ],
        scratch_shapes=[pltpu.VMEM((tokens, chans), jnp.bfloat16)] * 2,
        compiler_params=params(),
        cost_estimate=cost(10 * tokens * chans * chans, 12 * feats.size + 6 * wq.size),
        name="own_part",
    )(feats, wq, wk, wv, gq, gk)


def last_part(ids, counts, up, prev, down, feats, q, sums, norms, wk, wv, wo, gk):
    tokens, chans = feats.shape
    reach = up.shape[0] + prev.shape[0] + down.shape[0]
    smem = pl.BlockSpec(memory_space=pltpu.SMEM)
    vmem = pl.BlockSpec(memory_space=pltpu.VMEM)
    return pl.pallas_call(
        last_kernel,
        in_specs=[smem, smem] + [vmem] * 11,
        out_specs=vmem,
        out_shape=jax.ShapeDtypeStruct((tokens, chans), jnp.bfloat16),
        scratch_shapes=[pltpu.VMEM((reach, chans), jnp.bfloat16)] * 2
        + [pltpu.VMEM((tokens, chans), jnp.float32)] * 2,
        compiler_params=params(),
        cost_estimate=cost(16 * tokens * chans * chans, 20 * feats.size + 6 * wk.size),
        name="last_part",
    )(ids, counts, up, prev, down, feats, q, sums, norms, wk, wv, wo, gk)


def passed_on(array, axis, distance):
    devices = range(lax.axis_size(axis))
    return lax.ppermute(array, axis, [(i, i + distance) for i in devices if i + distance in devices])


def shards(
    frames_x, conv_weight, conv_bias, query_weight, key_weight, value_weight, out_weight,
    query_gain, key_gain, source_ids, valid_counts,
):
    _, band_rows, width, chans = frames_x.shape
    tokens = band_rows * width
    halo = DISP * BLOCK
    x = frames_x.reshape(tokens, chans)
    bias = conv_bias.reshape(1, chans)
    gq = query_gain.reshape(1, chans)
    gk = key_gain.reshape(1, chans)
    before = passed_on(x[tokens - BLOCK :], "row", 1)
    after = passed_on(x[:BLOCK], "row", -1)
    inner = conv_inner(x, conv_weight, bias)
    edges = conv_edge(before, x, after, conv_weight, bias)
    feats = jnp.concatenate([edges[:BLOCK], inner, edges[BLOCK:]], 0)
    prev = passed_on(feats, "frame", 1)
    q, sums, norms = own_part(feats, query_weight, key_weight, value_weight, gq, gk)
    up = passed_on(prev[tokens - halo :], "row", 1)
    down = passed_on(prev[:halo], "row", -1)
    frame_pos = lax.axis_index("frame")
    band_pos = lax.axis_index("row")
    ids = jnp.clip(source_ids[0] - (band_pos * band_rows - DISP), 0, band_rows + 2 * DISP - 1)
    counts = jnp.where(frame_pos > 0, valid_counts[0], 0)
    out = last_part(
        ids, counts, up, prev, down, feats, q, sums, norms, key_weight, value_weight, out_weight, gk
    )
    return out.reshape(1, band_rows, width, chans)


def solution(mesh):
    return jax.shard_map(
        shards,
        mesh=mesh,
        in_specs=(
            P("frame", "row", None, None),
            P(), P(), P(), P(), P(), P(), P(), P(),
            P("frame", "row", None),
            P("frame", "row"),
        ),
        out_specs=P("frame", "row", None, None),
        check_vma=False,
    )
```

```python
import jax
import jax.numpy as jnp
from jax import lax
from jax.experimental import pallas as pl
from jax.experimental.pallas import tpu as pltpu
from jax.sharding import PartitionSpec as P

HEADS = 8
HD = 64
KSRC = 4
BLOCK = 128
DISP = 2
PAIR = 2 * HD
VMEM_BYTES = 40 * 1024 * 1024

NT = (((1,), (1,)), ((), ()))


def dot(a, b):
    return jnp.dot(a, b, preferred_element_type=jnp.float32)


def from_left(y):
    column = lax.broadcasted_iota(jnp.int32, y.shape, 0) % BLOCK
    return jnp.where(column == 0, 0.0, pltpu.roll(y, 1, 0))


def from_right(y):
    column = lax.broadcasted_iota(jnp.int32, y.shape, 0) % BLOCK
    return jnp.where(column == BLOCK - 1, 0.0, pltpu.roll(y, y.shape[0] - 1, 0))


def row_of(index, count=1):
    return pl.ds(index * BLOCK, count * BLOCK)


def conv_inner_kernel(x_ref, w_hbm, b_ref, out_ref, w_ref, acc_ref, sems):
    rows = out_ref.shape[0] // BLOCK
    order = (1, 0, 2)
    copies = [
        pltpu.make_async_copy(w_hbm.at[:, c], w_ref.at[:, c], sems.at[c]) for c in range(3)
    ]
    for c in order:
        copies[c].start()
    for c in order:
        copies[c].wait()
        y = sum(dot(x_ref[row_of(a, rows)], w_ref[a, c]) for a in range(3))
        if c == 1:
            acc_ref[...] = y + b_ref[...]
        elif c == 0:
            acc_ref[...] += from_left(y)
        else:
            out_ref[...] = (acc_ref[...] + from_right(y)).astype(jnp.bfloat16)


def conv_edge_kernel(before_ref, x_ref, after_ref, inner_ref, w_ref, b_ref, outer_ref, mid_ref):
    rows = x_ref.shape[0] // BLOCK
    upper = [before_ref[...], x_ref[row_of(0)], x_ref[row_of(1)]]
    lower = [x_ref[row_of(rows - 2)], x_ref[row_of(rows - 1)], after_ref[...]]
    lines = [jnp.concatenate([upper[a], lower[a]], 0) for a in range(3)]
    left, mid, right = (sum(dot(lines[a], w_ref[a, c]) for a in range(3)) for c in range(3))
    total = from_left(left) + (mid + b_ref[...]) + from_right(right)
    total = total.astype(jnp.bfloat16)
    outer_ref[row_of(0)] = total[:BLOCK]
    outer_ref[row_of(2 * DISP - 1)] = total[BLOCK:]
    outer_ref[row_of(1, DISP - 1)] = inner_ref[row_of(0, DISP - 1)]
    outer_ref[row_of(DISP, DISP - 1)] = inner_ref[row_of(rows - 1 - DISP, DISP - 1)]
    mid_ref[...] = inner_ref[row_of(DISP - 1, rows - 2 * DISP)]


def head_norm(proj, gain):
    squares = (proj * proj).astype(jnp.bfloat16)
    wide = 4 * HD
    row = lax.broadcasted_iota(jnp.int32, (wide, wide), 0) // HD
    col = lax.broadcasted_iota(jnp.int32, (wide, wide), 1) // HD
    mean_of = jnp.where(row == col, 1.0 / HD, 0.0).astype(jnp.bfloat16)
    means = [dot(squares[:, i : i + wide], mean_of) for i in range(0, HEADS * HD, wide)]
    mean = jnp.concatenate(means, 1)
    return (proj * lax.rsqrt(mean + 1e-06) * gain).astype(jnp.bfloat16)


def pair_product(q, k, v, weights=None):
    low = lax.broadcasted_iota(jnp.int32, (BLOCK, PAIR), 1) < HD
    zero = jnp.zeros((BLOCK, PAIR), jnp.bfloat16)
    one = jnp.ones((BLOCK, PAIR), jnp.bfloat16)
    keys = jnp.concatenate([jnp.where(low, k, zero), jnp.where(low, zero, k)], 0)
    expo = jnp.exp(lax.dot_general(q, keys, NT, preferred_element_type=jnp.float32))
    if weights is not None:
        blocks = [expo[i * BLOCK : (i + 1) * BLOCK] * w for i, w in enumerate(weights)]
        expo = jnp.concatenate(blocks, 0)
    upper = jnp.concatenate([jnp.where(low, v, zero), jnp.where(low, one, zero)], 1)
    lower = jnp.concatenate([jnp.where(low, zero, v), jnp.where(low, zero, one)], 1)
    return dot(expo.astype(jnp.bfloat16), jnp.concatenate([upper, lower], 0))


def own_kernel(outer_ref, mid_ref, wq_ref, wk_ref, wv_ref, gq_ref, gk_ref, q_ref, acc_ref, k_ref, v_ref):
    reach = DISP * BLOCK
    inner = mid_ref.shape[0]
    pieces = ((outer_ref.at[:reach], 0), (mid_ref, reach), (outer_ref.at[reach:], reach + inner))
    for ref, start in pieces:
        feats = ref[...]
        rows = pl.ds(start, feats.shape[0])
        q_ref[rows] = head_norm(dot(feats, wq_ref[...]), gq_ref[...] * HD**-0.5)
        k_ref[rows] = head_norm(dot(feats, wk_ref[...]), gk_ref[...])
        v_ref[rows] = dot(feats, wv_ref[...]).astype(jnp.bfloat16)

    @pl.loop(0, q_ref.shape[0] // BLOCK)
    def _(block):
        rows = pl.ds(pl.multiple_of(block * BLOCK, BLOCK), BLOCK)
        for p in range(HEADS // 2):
            cols = pl.ds(p * PAIR, PAIR)
            acc_ref[rows, pl.ds(2 * p * PAIR, 2 * PAIR)] = pair_product(
                q_ref[rows, cols], k_ref[rows, cols], v_ref[rows, cols]
            )


def absorb(ids_ref, counts_ref, pieces, q_ref, acc_ref, wk_ref, wv_ref, gk_ref, k_ref, v_ref):
    rows = q_ref.shape[0] // BLOCK
    has_previous = lax.axis_index("frame") > 0
    first_row = lax.axis_index("row") * rows
    done = 0
    for ref, places in pieces:
        feats = ref[...]
        k_ref[row_of(done, len(places))] = head_norm(dot(feats, wk_ref[...]), gk_ref[...])
        v_ref[row_of(done, len(places))] = dot(feats, wv_ref[...]).astype(jnp.bfloat16)
        for i, place in enumerate(places):
            low, high = max(0, place - DISP), min(rows - 1, place + DISP)
            weights = []
            for r in range(low, high + 1):
                times = jnp.float32(0)
                for j in range(KSRC):
                    named = (ids_ref[r, j] == first_row + place) & (j < counts_ref[r]) & has_previous
                    times += jnp.where(named, jnp.float32(1), jnp.float32(0))
                weights.append(times)
            queries = row_of(low, high + 1 - low)
            source = row_of(done + i)
            for p in range(HEADS // 2):
                cols = pl.ds(p * PAIR, PAIR)
                acc_ref[queries, pl.ds(2 * p * PAIR, 2 * PAIR)] += pair_product(
                    q_ref[queries, cols], k_ref[source, cols], v_ref[source, cols], weights
                )
        done += len(places)


def outer_places(rows):
    return tuple(range(DISP)) + tuple(range(rows - DISP, rows))


def early_kernel(
    ids_ref, counts_ref, outer_ref, q_ref, acc_in_ref, wk_ref, wv_ref, gk_ref, acc_ref, k_ref, v_ref
):
    rows = q_ref.shape[0] // BLOCK
    acc_ref[...] = acc_in_ref[...]
    pieces = ((outer_ref, outer_places(rows)),)
    absorb(ids_ref, counts_ref, pieces, q_ref, acc_ref, wk_ref, wv_ref, gk_ref, k_ref, v_ref)


def halo_kernel(
    ids_ref, counts_ref, up_ref, down_ref, q_ref, acc_in_ref, wk_ref, wv_ref, gk_ref,
    acc_ref, k_ref, v_ref,
):
    rows = q_ref.shape[0] // BLOCK
    acc_ref[...] = acc_in_ref[...]
    pieces = ((up_ref, tuple(range(-DISP, 0))), (down_ref, tuple(range(rows, rows + DISP))))
    absorb(ids_ref, counts_ref, pieces, q_ref, acc_ref, wk_ref, wv_ref, gk_ref, k_ref, v_ref)


def late_kernel(
    ids_ref, counts_ref, mid_ref, q_ref, acc_in_ref, wk_ref, wv_ref, gk_ref,
    own_outer_ref, own_mid_ref, wo_ref, out_ref, acc_ref, k_ref, v_ref,
):
    rows = q_ref.shape[0] // BLOCK
    acc_ref[...] = acc_in_ref[...]
    pieces = ((mid_ref, tuple(range(DISP, rows - DISP))),)
    absorb(ids_ref, counts_ref, pieces, q_ref, acc_ref, wk_ref, wv_ref, gk_ref, k_ref, v_ref)
    parts = []
    for p in range(HEADS // 2):
        both = acc_ref[:, pl.ds(2 * p * PAIR, 2 * PAIR)]
        parts.append((both[:, :PAIR] / both[:, PAIR:]).astype(jnp.bfloat16))
    change = dot(jnp.concatenate(parts, 1), wo_ref[...])
    reach = DISP * BLOCK
    inner = own_mid_ref.shape[0]
    pieces = (
        (own_outer_ref.at[:reach], 0), (own_mid_ref, reach), (own_outer_ref.at[reach:], reach + inner),
    )
    for ref, start in pieces:
        feats = ref[...].astype(jnp.float32)
        stop = start + feats.shape[0]
        out_ref[start:stop] = (feats + change[start:stop]).astype(jnp.bfloat16)


SMEM = pl.BlockSpec(memory_space=pltpu.SMEM)
VMEM = pl.BlockSpec(memory_space=pltpu.VMEM)


def call(kernel, name, args, outs, scratch=(), specs=None, flops=0, aliases=None):
    moved = sum(a.size * a.dtype.itemsize for a in args)
    return pl.pallas_call(
        kernel,
        in_specs=specs or [VMEM] * len(args),
        out_specs=[VMEM] * len(outs),
        out_shape=[jax.ShapeDtypeStruct(shape, dtype) for shape, dtype in outs],
        scratch_shapes=list(scratch),
        input_output_aliases=aliases or {},
        compiler_params=pltpu.CompilerParams(vmem_limit_bytes=VMEM_BYTES),
        cost_estimate=pl.CostEstimate(flops=int(flops), bytes_accessed=int(moved), transcendentals=0),
        name=name,
    )(*args)


def passed_on(array, axis, distance):
    devices = range(lax.axis_size(axis))
    return lax.ppermute(array, axis, [(i, i + distance) for i in devices if i + distance in devices])


def shards(
    frames_x, conv_weight, conv_bias, query_weight, key_weight, value_weight, out_weight,
    query_gain, key_gain, source_ids, valid_counts,
):
    _, band_rows, width, chans = frames_x.shape
    tokens = band_rows * width
    reach = DISP * BLOCK
    x = frames_x.reshape(tokens, chans)
    bias = conv_bias.reshape(1, chans)
    gq = query_gain.reshape(1, chans)
    gk = key_gain.reshape(1, chans)
    ids, counts = source_ids[0], valid_counts[0]
    half, full = jnp.bfloat16, jnp.float32
    square = chans * chans

    before = passed_on(x[tokens - BLOCK :], "row", 1)
    after = passed_on(x[:BLOCK], "row", -1)
    (inner,) = call(
        conv_inner_kernel, "conv_inner", (x, conv_weight, bias), [((tokens - 2 * BLOCK, chans), half)],
        [
            pltpu.VMEM(conv_weight.shape, half),
            pltpu.VMEM((tokens - 2 * BLOCK, chans), full),
            pltpu.SemaphoreType.DMA((3,)),
        ],
        [VMEM, pl.BlockSpec(memory_space=pltpu.HBM), VMEM],
        18 * (tokens - 2 * BLOCK) * square,
    )
    outer, mid = call(
        conv_edge_kernel, "conv_edge", (before, x, after, inner, conv_weight, bias),
        [((2 * reach, chans), half), ((tokens - 2 * reach, chans), half)],
        flops=36 * BLOCK * square,
    )
    prev_outer = passed_on(outer, "frame", 1)
    prev_mid = passed_on(mid, "frame", 1)
    q, acc = call(
        own_kernel, "own_part", (outer, mid, query_weight, key_weight, value_weight, gq, gk),
        [((tokens, chans), half), ((tokens, 2 * chans), full)],
        [pltpu.VMEM((tokens, chans), half)] * 2,
        flops=10 * tokens * square,
    )
    prev_outer, q, acc = lax.optimization_barrier((prev_outer, q, acc))
    up = passed_on(prev_outer[reach:], "row", 1)
    down = passed_on(prev_outer[:reach], "row", -1)

    def keys_and_values(rows):
        return [pltpu.VMEM((rows * BLOCK, chans), half)] * 2

    weights = (key_weight, value_weight, gk)
    accs = [((tokens, 2 * chans), full)]
    (acc,) = call(
        early_kernel, "early_rows", (ids, counts, prev_outer, q, acc, *weights), accs,
        keys_and_values(2 * DISP), [SMEM] * 2 + [VMEM] * 6, 8 * tokens * square, {4: 0},
    )
    (acc,) = call(
        halo_kernel, "halo_rows", (ids, counts, up, down, q, acc, *weights), accs,
        keys_and_values(2 * DISP), [SMEM] * 2 + [VMEM] * 7, 4 * tokens * square, {5: 0},
    )
    (out,) = call(
        late_kernel, "late_rows", (ids, counts, prev_mid, q, acc, *weights, outer, mid, out_weight),
        [((tokens, chans), half)],
        [pltpu.VMEM((tokens, 2 * chans), full)] + keys_and_values(band_rows - 2 * DISP),
        [SMEM] * 2 + [VMEM] * 9, 8 * tokens * square,
    )
    return out.reshape(1, band_rows, width, chans)


def solution(mesh):
    return jax.shard_map(
        shards,
        mesh=mesh,
        in_specs=(
            P("frame", "row", None, None),
            P(), P(), P(), P(), P(), P(), P(), P(),
            P("frame", "row", None),
            P("frame", "row"),
        ),
        out_specs=P("frame", "row", None, None),
        check_vma=False,
    )
```

```python
import jax
import jax.numpy as jnp
from jax import lax
from jax.experimental import pallas as pl
from jax.experimental.pallas import tpu as pltpu
from jax.sharding import PartitionSpec as P

HEADS = 8
HD = 64
KSRC = 4
BLOCK = 128
DISP = 2
PAIR = 2 * HD

NT = (((1,), (1,)), ((), ()))


def dot(a, b):
    return jnp.dot(a, b, preferred_element_type=jnp.float32)


def from_left(y):
    column = lax.broadcasted_iota(jnp.int32, y.shape, 0) % BLOCK
    return jnp.where(column == 0, 0.0, pltpu.roll(y, 1, 0))


def from_right(y):
    column = lax.broadcasted_iota(jnp.int32, y.shape, 0) % BLOCK
    return jnp.where(column == BLOCK - 1, 0.0, pltpu.roll(y, y.shape[0] - 1, 0))


def row_of(index, count=1):
    return pl.ds(index * BLOCK, count * BLOCK)


def convolved(lines, w_ref, b_ref):
    left, mid, right = (sum(dot(lines(a), w_ref[a, c]) for a in range(3)) for c in range(3))
    return (from_left(left) + (mid + b_ref[...]) + from_right(right)).astype(jnp.bfloat16)


def conv_mid_kernel(x_ref, w_ref, b_ref, first_ref, last_ref, mid_ref):
    rows = mid_ref.shape[0] // BLOCK
    first_ref[...] = x_ref[row_of(0)]
    last_ref[...] = x_ref[row_of(rows + 2 * DISP - 1)]
    mid_ref[...] = convolved(lambda a: x_ref[row_of(DISP - 1 + a, rows)], w_ref, b_ref)


def conv_edge_kernel(before_ref, x_ref, after_ref, w_ref, b_ref, top_ref, bottom_ref):
    rows = x_ref.shape[0] // BLOCK
    held = DISP + 1
    upper = jnp.concatenate([before_ref[...], x_ref[row_of(0, held)]], 0)
    lower = jnp.concatenate([x_ref[row_of(rows - held, held)], after_ref[...]], 0)

    def lines(a):
        part = slice(a * BLOCK, (a + DISP) * BLOCK)
        return jnp.concatenate([upper[part], lower[part]], 0)

    total = convolved(lines, w_ref, b_ref)
    top_ref[...] = total[: DISP * BLOCK]
    bottom_ref[...] = total[DISP * BLOCK :]


def head_norm(proj, gain):
    squares = (proj * proj).astype(jnp.bfloat16)
    wide = 4 * HD
    row = lax.broadcasted_iota(jnp.int32, (wide, wide), 0) // HD
    col = lax.broadcasted_iota(jnp.int32, (wide, wide), 1) // HD
    mean_of = jnp.where(row == col, 1.0 / HD, 0.0).astype(jnp.bfloat16)
    means = [dot(squares[:, i : i + wide], mean_of) for i in range(0, HEADS * HD, wide)]
    mean = jnp.concatenate(means, 1)
    return (proj * lax.rsqrt(mean + 1e-06) * gain).astype(jnp.bfloat16)


def pair_product(q, k, v, weights=None):
    low = lax.broadcasted_iota(jnp.int32, (BLOCK, PAIR), 1) < HD
    zero = jnp.zeros((BLOCK, PAIR), jnp.bfloat16)
    one = jnp.ones((BLOCK, PAIR), jnp.bfloat16)
    keys = jnp.concatenate([jnp.where(low, k, zero), jnp.where(low, zero, k)], 0)
    expo = jnp.exp(lax.dot_general(q, keys, NT, preferred_element_type=jnp.float32))
    if weights is not None:
        blocks = [expo[i * BLOCK : (i + 1) * BLOCK] * w for i, w in enumerate(weights)]
        expo = jnp.concatenate(blocks, 0)
    upper = jnp.concatenate([jnp.where(low, v, zero), jnp.where(low, one, zero)], 1)
    lower = jnp.concatenate([jnp.where(low, zero, v), jnp.where(low, zero, one)], 1)
    return dot(expo.astype(jnp.bfloat16), jnp.concatenate([upper, lower], 0))


def band_pieces(top_ref, mid_ref, bottom_ref):
    reach = DISP * BLOCK
    return ((top_ref, 0), (mid_ref, reach), (bottom_ref, reach + mid_ref.shape[0]))


def own_kernel(
    top_ref, mid_ref, bottom_ref, wq_ref, wk_ref, wv_ref, gq_ref, gk_ref, q_ref, acc_ref, k_ref, v_ref
):
    pieces = band_pieces(top_ref, mid_ref, bottom_ref)
    for ref, start in pieces:
        feats = ref[...]
        rows = pl.ds(start, feats.shape[0])
        q_ref[rows] = head_norm(dot(feats, wq_ref[...]), gq_ref[...] * HD**-0.5)
        k_ref[rows] = head_norm(dot(feats, wk_ref[...]), gk_ref[...])
        v_ref[rows] = dot(feats, wv_ref[...]).astype(jnp.bfloat16)

    @pl.loop(0, q_ref.shape[0] // BLOCK)
    def _(block):
        rows = pl.ds(pl.multiple_of(block * BLOCK, BLOCK), BLOCK)
        for p in range(HEADS // 2):
            cols = pl.ds(p * PAIR, PAIR)
            acc_ref[rows, pl.ds(2 * p * PAIR, 2 * PAIR)] = pair_product(
                q_ref[rows, cols], k_ref[rows, cols], v_ref[rows, cols]
            )


def absorb(ids_ref, counts_ref, pieces, q_ref, acc_ref, wk_ref, wv_ref, gk_ref, k_ref, v_ref, base=0):
    rows = q_ref.shape[0] // BLOCK
    has_previous = lax.axis_index("frame") > 0
    first_row = lax.axis_index("row") * rows
    done = 0
    for ref, places in pieces:
        feats = ref[...]
        k_ref[row_of(done, len(places))] = head_norm(dot(feats, wk_ref[...]), gk_ref[...])
        v_ref[row_of(done, len(places))] = dot(feats, wv_ref[...]).astype(jnp.bfloat16)
        for i, place in enumerate(places):
            low, high = max(0, place - DISP), min(rows - 1, place + DISP)
            weights = []
            for r in range(low, high + 1):
                times = jnp.float32(0)
                for j in range(KSRC):
                    named = (ids_ref[r, j] == first_row + place) & (j < counts_ref[r]) & has_previous
                    times += jnp.where(named, jnp.float32(1), jnp.float32(0))
                weights.append(times)
            queries = row_of(low, high + 1 - low)
            sums = row_of(low - base, high + 1 - low)
            source = row_of(done + i)
            for p in range(HEADS // 2):
                cols = pl.ds(p * PAIR, PAIR)
                acc_ref[sums, pl.ds(2 * p * PAIR, 2 * PAIR)] += pair_product(
                    q_ref[queries, cols], k_ref[source, cols], v_ref[source, cols], weights
                )
        done += len(places)


def mid_kernel(
    ids_ref, counts_ref, prev_ref, q_ref, acc_in_ref, wk_ref, wv_ref, gk_ref, acc_ref, k_ref, v_ref
):
    rows = q_ref.shape[0] // BLOCK
    acc_ref[...] = acc_in_ref[...]
    pieces = ((prev_ref, tuple(range(DISP, rows - DISP))),)
    absorb(ids_ref, counts_ref, pieces, q_ref, acc_ref, wk_ref, wv_ref, gk_ref, k_ref, v_ref)


def top_kernel(
    ids_ref, counts_ref, prev_ref, q_ref, acc_in_ref, wk_ref, wv_ref, gk_ref, acc_ref, k_ref, v_ref
):
    acc_ref[...] = acc_in_ref[...]
    pieces = ((prev_ref, tuple(range(DISP))),)
    absorb(ids_ref, counts_ref, pieces, q_ref, acc_ref, wk_ref, wv_ref, gk_ref, k_ref, v_ref)


def finish(acc_ref, wo_ref, pieces, out_ref):
    parts = []
    for p in range(HEADS // 2):
        both = acc_ref[:, pl.ds(2 * p * PAIR, 2 * PAIR)]
        parts.append((both[:, :PAIR] / both[:, PAIR:]).astype(jnp.bfloat16))
    change = dot(jnp.concatenate(parts, 1), wo_ref[...])
    begin = 0
    for ref in pieces:
        feats = ref[...].astype(jnp.float32)
        stop = begin + feats.shape[0]
        out_ref[begin:stop] = (feats + change[begin:stop]).astype(jnp.bfloat16)
        begin = stop


def bottom_kernel(
    ids_ref, counts_ref, prev_ref, below_ref, q_ref, acc_in_ref, wk_ref, wv_ref, gk_ref,
    mid_ref, bottom_ref, wo_ref, out_hbm, acc_ref, k_ref, v_ref, out_ref, sem,
):
    rows = q_ref.shape[0] // BLOCK
    acc_ref[...] = acc_in_ref[DISP * BLOCK :]
    pieces = ((prev_ref, tuple(range(rows - DISP, rows))), (below_ref, tuple(range(rows, rows + DISP))))
    absorb(ids_ref, counts_ref, pieces, q_ref, acc_ref, wk_ref, wv_ref, gk_ref, k_ref, v_ref, DISP)
    finish(acc_ref, wo_ref, (mid_ref, bottom_ref), out_ref)
    copy = pltpu.make_async_copy(out_ref, out_hbm.at[row_of(DISP, rows - DISP)], sem)
    copy.start()
    copy.wait()


def last_kernel(
    ids_ref, counts_ref, above_ref, q_ref, acc_in_ref, wk_ref, wv_ref, gk_ref,
    top_ref, wo_ref, rest_hbm, out_hbm, acc_ref, k_ref, v_ref, out_ref, sem,
):
    del rest_hbm
    acc_ref[...] = acc_in_ref[: DISP * BLOCK]
    pieces = ((above_ref, tuple(range(-DISP, 0))),)
    absorb(ids_ref, counts_ref, pieces, q_ref, acc_ref, wk_ref, wv_ref, gk_ref, k_ref, v_ref)
    finish(acc_ref, wo_ref, (top_ref,), out_ref)
    copy = pltpu.make_async_copy(out_ref, out_hbm.at[row_of(0, DISP)], sem)
    copy.start()
    copy.wait()


SMEM = pl.BlockSpec(memory_space=pltpu.SMEM)
VMEM = pl.BlockSpec(memory_space=pltpu.VMEM)


HBM = pl.BlockSpec(memory_space=pltpu.HBM)
MEBI = 1024 * 1024


def call(kernel, name, args, outs, scratch=(), specs=None, aliases=None, limit=24, cost=2, out_specs=None):
    return pl.pallas_call(
        kernel,
        in_specs=specs or [VMEM] * len(args),
        out_specs=out_specs or [VMEM] * len(outs),
        out_shape=[jax.ShapeDtypeStruct(shape, dtype) for shape, dtype in outs],
        scratch_shapes=list(scratch),
        input_output_aliases=aliases or {},
        compiler_params=pltpu.CompilerParams(vmem_limit_bytes=limit * MEBI),
        cost_estimate=pl.CostEstimate(flops=cost * 1000000000, bytes_accessed=0, transcendentals=0),
        name=name,
    )(*args)


def passed_on(array, axis, distance):
    devices = range(lax.axis_size(axis))
    return lax.ppermute(array, axis, [(i, i + distance) for i in devices if i + distance in devices])


def shards(
    frames_x, conv_weight, conv_bias, query_weight, key_weight, value_weight, out_weight,
    query_gain, key_gain, source_ids, valid_counts,
):
    _, band_rows, width, chans = frames_x.shape
    tokens = band_rows * width
    reach = DISP * BLOCK
    x = frames_x.reshape(tokens, chans)
    bias = conv_bias.reshape(1, chans)
    gq = query_gain.reshape(1, chans)
    gk = key_gain.reshape(1, chans)
    ids, counts = source_ids[0], valid_counts[0]
    half, full = jnp.bfloat16, jnp.float32
    dma = pltpu.SemaphoreType.DMA

    first, last, mid = call(
        conv_mid_kernel, "conv_mid", (x, conv_weight, bias),
        [((BLOCK, chans), half), ((BLOCK, chans), half), ((tokens - 2 * reach, chans), half)],
        cost=2,
    )
    before = passed_on(last, "row", 1)
    after = passed_on(first, "row", -1)
    top, bottom = call(
        conv_edge_kernel, "conv_edge", (before, x, after, conv_weight, bias),
        [((reach, chans), half)] * 2,
        cost=0,
    )
    prev_mid = passed_on(mid, "frame", 1)
    prev_top = passed_on(top, "frame", 1)
    q, acc = call(
        own_kernel, "own_part", (top, mid, bottom, query_weight, key_weight, value_weight, gq, gk),
        [((tokens, chans), half), ((tokens, 2 * chans), full)],
        [pltpu.VMEM((tokens, chans), half)] * 2,
    )
    bottom, q = lax.optimization_barrier((bottom, q))
    prev_bottom = passed_on(bottom, "frame", 1)

    def keys_and_values(rows):
        return [pltpu.VMEM((rows * BLOCK, chans), half)] * 2

    weights = (key_weight, value_weight, gk)
    accs = [((tokens, 2 * chans), full)]
    (acc,) = call(
        mid_kernel, "mid_rows", (ids, counts, prev_mid, q, acc, *weights), accs,
        keys_and_values(band_rows - 2 * DISP), [SMEM] * 2 + [VMEM] * 6, {4: 0}, cost=40,
    )
    prev_top, acc = lax.optimization_barrier((prev_top, acc))
    below = passed_on(prev_top, "row", -1)
    (acc,) = call(
        top_kernel, "top_rows", (ids, counts, prev_top, q, acc, *weights), accs,
        keys_and_values(DISP), [SMEM] * 2 + [VMEM] * 6, {4: 0},
    )
    prev_bottom, acc = lax.optimization_barrier((prev_bottom, acc))
    above = passed_on(prev_bottom, "row", 1)
    outs = [((tokens, chans), half)]
    (out,) = call(
        bottom_kernel, "bottom_rows",
        (ids, counts, prev_bottom, below, q, acc, *weights, mid, bottom, out_weight), outs,
        [pltpu.VMEM((tokens - reach, 2 * chans), full)] + keys_and_values(2 * DISP)
        + [pltpu.VMEM((tokens - reach, chans), half), dma(())],
        [SMEM] * 2 + [VMEM] * 10, out_specs=[HBM],
    )
    (out,) = call(
        last_kernel, "last_rows", (ids, counts, above, q, acc, *weights, top, out_weight, out), outs,
        [pltpu.VMEM((reach, 2 * chans), full)] + keys_and_values(DISP)
        + [pltpu.VMEM((reach, chans), half), dma(())],
        [SMEM] * 2 + [VMEM] * 8 + [HBM], {10: 0}, out_specs=[HBM],
    )
    return out.reshape(1, band_rows, width, chans)


def solution(mesh):
    return jax.shard_map(
        shards,
        mesh=mesh,
        in_specs=(
            P("frame", "row", None, None),
            P(), P(), P(), P(), P(), P(), P(), P(),
            P("frame", "row", None),
            P("frame", "row"),
        ),
        out_specs=P("frame", "row", None, None),
        check_vma=False,
    )
```

```python
import jax
import jax.numpy as jnp
from jax import lax
from jax.experimental import pallas as pl
from jax.experimental.pallas import tpu as pltpu
from jax.sharding import PartitionSpec as P

HEADS = 8
HD = 64
KSRC = 4
BLOCK = 128
DISP = 2
PAIR = 2 * HD

NT = (((1,), (1,)), ((), ()))


def dot(a, b):
    return jnp.dot(a, b, preferred_element_type=jnp.float32)


def from_left(y):
    column = lax.broadcasted_iota(jnp.int32, y.shape, 0) % BLOCK
    return jnp.where(column == 0, 0.0, pltpu.roll(y, 1, 0))


def from_right(y):
    column = lax.broadcasted_iota(jnp.int32, y.shape, 0) % BLOCK
    return jnp.where(column == BLOCK - 1, 0.0, pltpu.roll(y, y.shape[0] - 1, 0))


def row_of(index, count=1):
    return pl.ds(index * BLOCK, count * BLOCK)


def convolved(lines, w_ref, b_ref):
    left, mid, right = (sum(dot(lines(a), w_ref[a, c]) for a in range(3)) for c in range(3))
    return (from_left(left) + (mid + b_ref[...]) + from_right(right)).astype(jnp.bfloat16)


def weight_copies(w_hbm, w_ref, sems):
    return [
        [pltpu.make_async_copy(w_hbm.at[a, c], w_ref.at[a, c], sems.at[a, c]) for a in range(3)]
        for c in (1, 0, 2)
    ]


def start(copies):
    for copy in copies:
        copy.start()


def wait(copies):
    for copy in copies:
        copy.wait()


def column_sum(lines, w_ref, c):
    return sum(dot(lines(a), w_ref[a, c]) for a in range(3))


def streamed_columns(lines, w_hbm, w_ref, sems, ready):
    mid, left, right = weight_copies(w_hbm, w_ref, sems)
    start(mid)
    ready()
    start(left)
    wait(mid)
    y_mid = column_sum(lines, w_ref, 1)
    start(right)
    wait(left)
    y_left = column_sum(lines, w_ref, 0)
    wait(right)
    return y_left, y_mid, column_sum(lines, w_ref, 2)


def conv_mid_kernel(x_hbm, w_hbm, b_hbm, first_ref, last_ref, mid_ref, x_ref, w_ref, b_ref, sems, x_sems):
    rows = mid_ref.shape[0] // BLOCK
    inputs = [
        pltpu.make_async_copy(x_hbm, x_ref, x_sems.at[0]),
        pltpu.make_async_copy(b_hbm, b_ref, x_sems.at[1]),
    ]

    def ready():
        wait(inputs)
        first_ref[...] = x_ref[row_of(0)]
        last_ref[...] = x_ref[row_of(rows + 2 * DISP - 1)]

    def lines(a):
        return x_ref[row_of(DISP - 1 + a, rows)]

    start(inputs)
    left, mid, right = streamed_columns(lines, w_hbm, w_ref, sems, ready)
    mid_ref[...] = (from_left(left) + (mid + b_ref[...]) + from_right(right)).astype(jnp.bfloat16)


def conv_edge_kernel(before_ref, x_ref, after_ref, w_ref, b_ref, top_ref, bottom_ref):
    rows = x_ref.shape[0] // BLOCK
    held = DISP + 1
    upper = jnp.concatenate([before_ref[...], x_ref[row_of(0, held)]], 0)
    lower = jnp.concatenate([x_ref[row_of(rows - held, held)], after_ref[...]], 0)

    def lines(a):
        part = slice(a * BLOCK, (a + DISP) * BLOCK)
        return jnp.concatenate([upper[part], lower[part]], 0)

    total = convolved(lines, w_ref, b_ref)
    top_ref[...] = total[: DISP * BLOCK]
    bottom_ref[...] = total[DISP * BLOCK :]


def head_norm(proj, gain):
    squares = (proj * proj).astype(jnp.bfloat16)
    wide = 4 * HD
    row = lax.broadcasted_iota(jnp.int32, (wide, wide), 0) // HD
    col = lax.broadcasted_iota(jnp.int32, (wide, wide), 1) // HD
    mean_of = jnp.where(row == col, 1.0 / HD, 0.0).astype(jnp.bfloat16)
    means = [dot(squares[:, i : i + wide], mean_of) for i in range(0, HEADS * HD, wide)]
    mean = jnp.concatenate(means, 1)
    return (proj * lax.rsqrt(mean + 1e-06) * gain).astype(jnp.bfloat16)


def pair_product(q, k, v, weights=None):
    low = lax.broadcasted_iota(jnp.int32, (BLOCK, PAIR), 1) < HD
    zero = jnp.zeros((BLOCK, PAIR), jnp.bfloat16)
    one = jnp.ones((BLOCK, PAIR), jnp.bfloat16)
    keys = jnp.concatenate([jnp.where(low, k, zero), jnp.where(low, zero, k)], 0)
    expo = jnp.exp(lax.dot_general(q, keys, NT, preferred_element_type=jnp.float32))
    if weights is not None:
        blocks = [expo[i * BLOCK : (i + 1) * BLOCK] * w for i, w in enumerate(weights)]
        expo = jnp.concatenate(blocks, 0)
    upper = jnp.concatenate([jnp.where(low, v, zero), jnp.where(low, one, zero)], 1)
    lower = jnp.concatenate([jnp.where(low, zero, v), jnp.where(low, zero, one)], 1)
    return dot(expo.astype(jnp.bfloat16), jnp.concatenate([upper, lower], 0))


def band_pieces(top_ref, mid_ref, bottom_ref):
    reach = DISP * BLOCK
    return ((top_ref, 0), (mid_ref, reach), (bottom_ref, reach + mid_ref.shape[0]))


def own_kernel(
    top_ref, mid_ref, bottom_ref, wq_ref, wk_ref, wv_ref, gq_ref, gk_ref, q_ref, acc_ref, k_ref, v_ref
):
    pieces = band_pieces(top_ref, mid_ref, bottom_ref)
    for ref, start in pieces:
        feats = ref[...]
        rows = pl.ds(start, feats.shape[0])
        q_ref[rows] = head_norm(dot(feats, wq_ref[...]), gq_ref[...] * HD**-0.5)
        k_ref[rows] = head_norm(dot(feats, wk_ref[...]), gk_ref[...])
        v_ref[rows] = dot(feats, wv_ref[...]).astype(jnp.bfloat16)

    @pl.loop(0, q_ref.shape[0] // BLOCK)
    def _(block):
        rows = pl.ds(pl.multiple_of(block * BLOCK, BLOCK), BLOCK)
        for p in range(HEADS // 2):
            cols = pl.ds(p * PAIR, PAIR)
            acc_ref[rows, pl.ds(2 * p * PAIR, 2 * PAIR)] = pair_product(
                q_ref[rows, cols], k_ref[rows, cols], v_ref[rows, cols]
            )


def spans_of(fresh, low, high):
    spans = []
    for row in range(low, high):
        if spans and spans[-1][2] == fresh[row]:
            spans[-1] = (spans[-1][0], spans[-1][1] + 1, fresh[row])
        else:
            spans.append((row, 1, fresh[row]))
    return spans


def absorb(ids_ref, counts_ref, pieces, q_ref, acc_in_ref, acc_ref, wk_ref, wv_ref, gk_ref, k_ref, v_ref, base=0):
    fresh = [True] * (acc_ref.shape[0] // BLOCK)
    rows = q_ref.shape[0] // BLOCK
    has_previous = lax.axis_index("frame") > 0
    first_row = lax.axis_index("row") * rows
    done = 0
    for ref, places in pieces:
        feats = ref[...]
        k_ref[row_of(done, len(places))] = head_norm(dot(feats, wk_ref[...]), gk_ref[...])
        v_ref[row_of(done, len(places))] = dot(feats, wv_ref[...]).astype(jnp.bfloat16)
        for i, place in enumerate(places):
            low, high = max(0, place - DISP), min(rows - 1, place + DISP)
            weights = []
            for r in range(low, high + 1):
                times = jnp.float32(0)
                for j in range(KSRC):
                    named = (ids_ref[r, j] == first_row + place) & (j < counts_ref[r]) & has_previous
                    times += jnp.where(named, jnp.float32(1), jnp.float32(0))
                weights.append(times)
            queries = row_of(low, high + 1 - low)
            spans = spans_of(fresh, low - base, high + 1 - base)
            source = row_of(done + i)
            for p in range(HEADS // 2):
                cols = pl.ds(p * PAIR, PAIR)
                both = pair_product(
                    q_ref[queries, cols], k_ref[source, cols], v_ref[source, cols], weights
                )
                both_cols = pl.ds(2 * p * PAIR, 2 * PAIR)
                begin = 0
                for row, count, first_time in spans:
                    so_far = acc_in_ref if first_time else acc_ref
                    stop = begin + count * BLOCK
                    here = row_of(row, count)
                    acc_ref[here, both_cols] = (
                        so_far[row_of(row + base, count), both_cols] if first_time
                        else so_far[here, both_cols]
                    ) + both[begin:stop]
                    begin = stop
            for row in range(low - base, high + 1 - base):
                fresh[row] = False
        done += len(places)
    for row, waiting in enumerate(fresh):
        if waiting:
            acc_ref[row_of(row)] = acc_in_ref[row_of(row + base)]


def mid_kernel(
    ids_ref, counts_ref, prev_ref, q_ref, acc_in_ref, wk_ref, wv_ref, gk_ref, acc_ref, k_ref, v_ref
):
    rows = q_ref.shape[0] // BLOCK
    pieces = ((prev_ref, tuple(range(DISP, rows - DISP))),)
    absorb(ids_ref, counts_ref, pieces, q_ref, acc_in_ref, acc_ref, wk_ref, wv_ref, gk_ref, k_ref, v_ref)


def top_kernel(
    ids_ref, counts_ref, prev_ref, q_ref, acc_in_ref, wk_ref, wv_ref, gk_ref, acc_ref, k_ref, v_ref
):
    pieces = ((prev_ref, tuple(range(DISP))),)
    absorb(ids_ref, counts_ref, pieces, q_ref, acc_in_ref, acc_ref, wk_ref, wv_ref, gk_ref, k_ref, v_ref)


def finish(acc_ref, wo_ref, pieces, out_ref):
    parts = []
    for p in range(HEADS // 2):
        both = acc_ref[:, pl.ds(2 * p * PAIR, 2 * PAIR)]
        norm = both[:, PAIR:]
        guess = pl.reciprocal(norm, approx=True)
        parts.append((both[:, :PAIR] * (guess * (2.0 - norm * guess))).astype(jnp.bfloat16))
    change = dot(jnp.concatenate(parts, 1), wo_ref[...])
    begin = 0
    for ref in pieces:
        feats = ref[...].astype(jnp.float32)
        stop = begin + feats.shape[0]
        out_ref[begin:stop] = (feats + change[begin:stop]).astype(jnp.bfloat16)
        begin = stop


def bottom_kernel(
    ids_ref, counts_ref, prev_ref, below_ref, q_ref, acc_in_ref, wk_ref, wv_ref, gk_ref,
    mid_ref, bottom_ref, wo_ref, out_hbm, acc_ref, k_ref, v_ref, out_ref, sem,
):
    rows = q_ref.shape[0] // BLOCK
    pieces = ((prev_ref, tuple(range(rows - DISP, rows))), (below_ref, tuple(range(rows, rows + DISP))))
    absorb(ids_ref, counts_ref, pieces, q_ref, acc_in_ref, acc_ref, wk_ref, wv_ref, gk_ref, k_ref, v_ref, DISP)
    finish(acc_ref, wo_ref, (mid_ref, bottom_ref), out_ref)
    copy = pltpu.make_async_copy(out_ref, out_hbm.at[row_of(DISP, rows - DISP)], sem)
    copy.start()
    copy.wait()


def last_kernel(
    ids_ref, counts_ref, above_ref, q_ref, acc_in_ref, wk_ref, wv_ref, gk_ref,
    top_ref, wo_ref, rest_hbm, out_hbm, acc_ref, k_ref, v_ref, out_ref, sem,
):
    del rest_hbm
    pieces = ((above_ref, tuple(range(-DISP, 0))),)
    absorb(ids_ref, counts_ref, pieces, q_ref, acc_in_ref, acc_ref, wk_ref, wv_ref, gk_ref, k_ref, v_ref)
    finish(acc_ref, wo_ref, (top_ref,), out_ref)
    copy = pltpu.make_async_copy(out_ref, out_hbm.at[row_of(0, DISP)], sem)
    copy.start()
    copy.wait()


SMEM = pl.BlockSpec(memory_space=pltpu.SMEM)
VMEM = pl.BlockSpec(memory_space=pltpu.VMEM)


HBM = pl.BlockSpec(memory_space=pltpu.HBM)
MEBI = 1024 * 1024


def call(kernel, name, args, outs, scratch=(), specs=None, aliases=None, limit=24, cost=2, out_specs=None):
    return pl.pallas_call(
        kernel,
        in_specs=specs or [VMEM] * len(args),
        out_specs=out_specs or [VMEM] * len(outs),
        out_shape=[jax.ShapeDtypeStruct(shape, dtype) for shape, dtype in outs],
        scratch_shapes=list(scratch),
        input_output_aliases=aliases or {},
        compiler_params=pltpu.CompilerParams(vmem_limit_bytes=limit * MEBI),
        cost_estimate=pl.CostEstimate(flops=cost * 1000000000, bytes_accessed=0, transcendentals=0),
        name=name,
    )(*args)


def passed_on(array, axis, distance):
    devices = range(lax.axis_size(axis))
    return lax.ppermute(array, axis, [(i, i + distance) for i in devices if i + distance in devices])


def shards(
    frames_x, conv_weight, conv_bias, query_weight, key_weight, value_weight, out_weight,
    query_gain, key_gain, source_ids, valid_counts,
):
    _, band_rows, width, chans = frames_x.shape
    tokens = band_rows * width
    reach = DISP * BLOCK
    x = frames_x.reshape(tokens, chans)
    bias = conv_bias.reshape(1, chans)
    gq = query_gain.reshape(1, chans)
    gk = key_gain.reshape(1, chans)
    ids, counts = source_ids[0], valid_counts[0]
    half, full = jnp.bfloat16, jnp.float32
    dma = pltpu.SemaphoreType.DMA

    first, last, mid = call(
        conv_mid_kernel, "conv_mid", (x, conv_weight, bias),
        [((BLOCK, chans), half), ((BLOCK, chans), half), ((tokens - 2 * reach, chans), half)],
        [
            pltpu.VMEM((tokens, chans), half), pltpu.VMEM(conv_weight.shape, half),
            pltpu.VMEM(bias.shape, full), dma((3, 3)), dma((2,)),
        ],
        [HBM, HBM, HBM], limit=58, cost=2,
    )
    before = passed_on(last, "row", 1)
    after = passed_on(first, "row", -1)
    top, bottom = call(
        conv_edge_kernel, "conv_edge", (before, x, after, conv_weight, bias),
        [((reach, chans), half)] * 2,
        cost=0,
    )
    prev_mid = passed_on(mid, "frame", 1)
    prev_top = passed_on(top, "frame", 1)
    q, acc = call(
        own_kernel, "own_part", (top, mid, bottom, query_weight, key_weight, value_weight, gq, gk),
        [((tokens, chans), half), ((tokens, 2 * chans), full)],
        [pltpu.VMEM((tokens, chans), half)] * 2,
    )
    bottom, q = lax.optimization_barrier((bottom, q))
    prev_bottom = passed_on(bottom, "frame", 1)

    def keys_and_values(rows):
        return [pltpu.VMEM((rows * BLOCK, chans), half)] * 2

    weights = (key_weight, value_weight, gk)
    accs = [((tokens, 2 * chans), full)]
    (acc,) = call(
        mid_kernel, "mid_rows", (ids, counts, prev_mid, q, acc, *weights), accs,
        keys_and_values(band_rows - 2 * DISP), [SMEM] * 2 + [VMEM] * 6, {4: 0}, cost=40,
    )
    prev_top, acc = lax.optimization_barrier((prev_top, acc))
    below = passed_on(prev_top, "row", -1)
    (acc,) = call(
        top_kernel, "top_rows", (ids, counts, prev_top, q, acc, *weights), accs,
        keys_and_values(DISP), [SMEM] * 2 + [VMEM] * 6, {4: 0},
    )
    prev_bottom, acc = lax.optimization_barrier((prev_bottom, acc))
    above = passed_on(prev_bottom, "row", 1)
    outs = [((tokens, chans), half)]
    (out,) = call(
        bottom_kernel, "bottom_rows",
        (ids, counts, prev_bottom, below, q, acc, *weights, mid, bottom, out_weight), outs,
        [pltpu.VMEM((tokens - reach, 2 * chans), full)] + keys_and_values(2 * DISP)
        + [pltpu.VMEM((tokens - reach, chans), half), dma(())],
        [SMEM] * 2 + [VMEM] * 10, out_specs=[HBM],
    )
    (out,) = call(
        last_kernel, "last_rows", (ids, counts, above, q, acc, *weights, top, out_weight, out), outs,
        [pltpu.VMEM((reach, 2 * chans), full)] + keys_and_values(DISP)
        + [pltpu.VMEM((reach, chans), half), dma(())],
        [SMEM] * 2 + [VMEM] * 8 + [HBM], {10: 0}, out_specs=[HBM],
    )
    return out.reshape(1, band_rows, width, chans)


def solution(mesh):
    return jax.shard_map(
        shards,
        mesh=mesh,
        in_specs=(
            P("frame", "row", None, None),
            P(), P(), P(), P(), P(), P(), P(), P(),
            P("frame", "row", None),
            P("frame", "row"),
        ),
        out_specs=P("frame", "row", None, None),
        check_vma=False,
    )
```
